256 devices in a mesh: frames: 64 (over y, x_hi, z), heads: 4 (over x_lo, core).
Axes of the slice: x: 4 (x_hi: 2, x_lo: 2; x = x_hi * 2 + x_lo), y: 4, z: 8, core: 2. Of those that a mesh axis runs over, the one named last changes fastest.
Arguments:
- span_q: bfloat16 [32768, 5120], P('frames', 'heads'), may hold values from -6 to 6
- span_k: bfloat16 [32768, 5120], P('frames', 'heads'), may hold values from -6 to 6
- span_v: bfloat16 [32768, 5120], P('frames', 'heads'), may hold values from -6 to 6
- q_gain: float32 [5120], P('heads'), may hold values from 1 to 3
- k_gain: float32 [5120], P('heads'), may hold values from 0.5 to 2
- kv_cache: bfloat16 [128, 2, 128, 5120], P('frames', None, None, 'heads'), may hold values from -6 to 6
- frame_home: int32 [128], replicated, may hold values from 0 to 127, each once
- chosen_frames: int32 [5], replicated, may hold values from 0 to 127, as said below
Outputs:
- attended: bfloat16 [32768, 5120], P('frames', 'heads')
The draws below stay inside these ranges and needn't reach their ends.
Inputs may be any that keep to these rules, and one draw needn't show every extreme that they name: A permutation: frame i of the history is kept in row frame_home[i] of kv_cache. `chosen_frames`: 2 distinct key frames below 125, then the 3 most recent frames 128 - 3 to 127 in order.
All inputs are finite; a program needn't handle non-finite values.
Results may differ from the reference program's by a relative error of at most 0.012.
Values may be sent and summed in bfloat16 or wider, within the bound.
No kernel may reach another device: no remote copies, remote signals or barrier semaphores. Data moves between devices by JAX's collectives and lax.ppermute only.
A program may use at most 128 MiB of HBM per device.

```python
import math
import jax
import jax.numpy as jnp
from jax import lax

D = 5120
HEADS = 40
HD = 128
FT = 128
RECENT = 3
KEYS = 2
NF = 128
CANDIDATES = 8
SPAN = 4096
TOKENS = 32768


def draw_chosen_frames(key, part):
    key = jax.random.fold_in(key, 7)
    key_frames = jax.random.permutation(key, NF - RECENT)[:KEYS].astype(jnp.int32)
    recent = NF - RECENT + jnp.arange(RECENT, dtype=jnp.int32)
    return jnp.concatenate([key_frames, recent])


def block_levels(rng, shape, pieces, least, high):
    gain, own = 1.0, jax.random.fold_in(rng, 6)
    for dim, parts in pieces:
        draws = jnp.exp(jax.random.uniform(jax.random.fold_in(own, dim), (parts,), jnp.float32, least / len(pieces), high / len(pieces)))
        gain = gain * jnp.repeat(draws, shape[dim] // parts).reshape([-1 if axis == dim else 1 for axis in range(len(shape))])
    return gain


def gaussian(key, extent, scale, reach, cuts=(), kind=jnp.bfloat16):
    entries = jax.random.normal(key, extent, jnp.float32) * scale
    if len(cuts) > 0:
        entries = block_levels(key, extent, cuts, -0.22, 0.18) * entries
    return jnp.clip(entries, min=-reach, max=reach).astype(kind)


def setup_inputs(seed: int = 0) -> dict:
    streams_of = jax.random.split(jax.random.key(seed), 9)
    return {
        "span_q": gaussian(streams_of[0], (TOKENS, D), 1.0, 6.0, ((0, 64), (1, 4))),
        "span_k": gaussian(streams_of[1], (TOKENS, D), 1.0, 6.0, ((0, 64), (1, 4))),
        "span_v": gaussian(streams_of[2], (TOKENS, D), 1.0, 6.0, ((0, 64), (1, 4))),
        "q_gain": jnp.clip(jnp.exp(math.log(3.0) - 1.0986123 * jax.random.uniform(streams_of[3], (D,), jnp.float32) ** block_levels(streams_of[3], (D,), ((0, 4),), -0.2, 0.2)), 1.0, 3.0),
        "k_gain": jnp.clip(jnp.exp(math.log(2.0) - 1.3862944 * jax.random.uniform(streams_of[4], (D,), jnp.float32) ** block_levels(streams_of[4], (D,), ((0, 4),), -0.2, 0.2)), 0.5, 2.0),
        "kv_cache": gaussian(streams_of[5], (NF, 2, FT, D), 1.0, 6.0, ((0, 64), (3, 4))),
        "frame_home": jax.random.permutation(streams_of[6], NF).astype(jnp.int32),
        "chosen_frames": draw_chosen_frames(jax.random.fold_in(streams_of[8], 71), 0),
    }


logit_cap = 30.0

def rms_norm(matrix, gain_vector):
    values = matrix.astype(jnp.float32)
    inverse = lax.rsqrt(lax.optimization_barrier(jnp.mean(values * values, axis=-1, keepdims=True)) + 1e-06)
    return (values * inverse * gain_vector.astype(jnp.float32)).astype(jnp.bfloat16)

def reference(span_q, span_k, span_v, q_gain, k_gain, kv_cache, frame_home, chosen_frames):
    queries = rms_norm(span_q, q_gain)
    keys_new = rms_norm(span_k, k_gain)
    locations = frame_home[chosen_frames]
    picked = jnp.take(kv_cache, locations, axis=0)
    cache_keys = picked[:, 0].reshape(-1, D)
    cache_values = picked[:, 1].reshape(-1, D)

    def one_candidate(first_row):
        query_rows = lax.dynamic_slice_in_dim(queries, first_row, SPAN, 0)
        all_keys = jnp.concatenate([cache_keys, lax.dynamic_slice_in_dim(keys_new, first_row, SPAN, 0)], axis=0)
        all_values = jnp.concatenate([cache_values, lax.dynamic_slice_in_dim(span_v, first_row, SPAN, 0)], axis=0)

        def one_head(first_column):
            query_head = lax.dynamic_slice_in_dim(query_rows, first_column, HD, 1).astype(jnp.float32)
            key_head = lax.dynamic_slice_in_dim(all_keys, first_column, HD, 1).astype(jnp.float32)
            value_head = lax.dynamic_slice_in_dim(all_values, first_column, HD, 1).astype(jnp.float32)
            scores = jnp.dot(query_head, key_head.T, precision=lax.Precision.HIGHEST) * (1.0 / math.sqrt(HD))
            capped = logit_cap * jnp.tanh(scores / logit_cap)
            weights = jnp.exp(capped - logit_cap).astype(jnp.bfloat16).astype(jnp.float32)
            numerator = jnp.dot(weights, value_head, precision=lax.Precision.HIGHEST)
            denominator = lax.optimization_barrier(jnp.sum(weights, axis=-1, keepdims=True))
            return (numerator / denominator).astype(jnp.bfloat16)
        per_head = lax.map(one_head, jnp.arange(HEADS, dtype=jnp.int32) * HD)
        return per_head.transpose(1, 0, 2).reshape(SPAN, D)
    per_candidate = lax.map(one_candidate, jnp.arange(CANDIDATES, dtype=jnp.int32) * SPAN)
    return per_candidate.reshape(TOKENS, D)
```

```python
import functools
import math

import jax
import jax.numpy as jnp
from jax import lax
from jax.experimental import pallas as pl
from jax.experimental.pallas import tpu as pltpu
from jax.sharding import Mesh, PartitionSpec as P

D = 5120
HD = 128
SEL = 5
CAND = 8
ZED = 8
GROUP = 4
MAIN = ZED * HD
CAP = 30.0
LOG2E = math.log2(math.e)
PARTS = (("m", 0, 128), ("m", 128, 128), ("l", 0, 128), ("m", 256, 128), ("m", 384, 128))


def attend_kernel(q_ref, k_ref, v_ref, kc_ref, vc_ref, o_ref):
    q = q_ref[...]
    total = None
    for keys, values in ((k_ref, v_ref), (kc_ref, vc_ref)):
        scores = lax.dot_general(
            q, keys[...], (((1,), (1,)), ((), ())), preferred_element_type=jnp.float32
        )
        capped = jnp.tanh(scores * (1.0 / (CAP * math.sqrt(HD))))
        weights = jnp.exp2(capped * (CAP * LOG2E) - CAP * LOG2E).astype(jnp.bfloat16)
        term = jnp.dot(weights, values[...], preferred_element_type=jnp.float32)
        total = term if total is None else total + term
    o_ref[...] = (total[:, :HD] / total[:, HD:]).astype(jnp.bfloat16)


def attend(q, k, v, kc, vc, block=512):
    rows, keys, cached = q.shape[0], k.shape[0], kc.shape[0]
    whole = lambda n, w: pl.BlockSpec((n, w), lambda i: (0, 0))
    return pl.pallas_call(
        attend_kernel,
        grid=(rows // block,),
        in_specs=[
            pl.BlockSpec((block, HD), lambda i: (i, 0)),
            whole(keys, HD),
            whole(keys, 2 * HD),
            whole(cached, HD),
            whole(cached, 2 * HD),
        ],
        out_specs=pl.BlockSpec((block, HD), lambda i: (i, 0)),
        out_shape=jax.ShapeDtypeStruct((rows, HD), jnp.bfloat16),
        compiler_params=pltpu.CompilerParams(vmem_limit_bytes=48 * 2**20),
        cost_estimate=pl.CostEstimate(
            flops=2 * rows * (keys + cached) * 3 * HD * 2,
            bytes_accessed=2 * (2 * rows + 3 * (keys + cached)) * HD,
            transcendentals=2 * rows * (keys + cached),
        ),
    )(q, k, v, kc, vc)


def to_heads(x):
    return lax.all_to_all(x, "z", 1, 0, tiled=True)


def with_ones(v):
    return jnp.concatenate([v, jnp.ones_like(v)], axis=1)


def cached_frames(kv_cache, locations):
    main = lax.all_to_all(kv_cache[..., :MAIN], "cand", 2, 0, tiled=True)
    left = lax.all_to_all(kv_cache[..., MAIN:], "h", 2, 3, tiled=True)
    left = lax.all_to_all(left, "cand", 2, 0, tiled=True)
    home = locations // 2
    slot = (home // ZED) * 2 + locations % 2
    mine = (home % ZED == lax.axis_index("z"))[:, None, None, None]
    pieces = []
    for part in (main, left):
        picked = jnp.stack([lax.dynamic_index_in_dim(part, slot[s], 0, keepdims=False) for s in range(SEL)])
        picked = jnp.where(mine, picked, jnp.zeros_like(picked))
        pieces.append(picked.reshape(-1, MAIN))
    rows = jnp.concatenate(pieces, axis=0)
    rows = rows.reshape(-1, ZED, HD).transpose(1, 0, 2)
    rows = lax.psum_scatter(rows, "z", scatter_dimension=0, tiled=True)[0]
    every = lax.all_gather(rows, "cand", axis=0)
    count = SEL * 2 * 16
    main = every[:, :count].reshape(CAND, SEL, 2, 16, HD)
    left = lax.all_gather(every[:, count:], "h", axis=0).reshape(GROUP, CAND, SEL, 2, 4, HD)
    return (
        main[:, :, 0].reshape(-1, HD),
        main[:, :, 1].reshape(-1, HD),
        left[:, :, :, 0].reshape(-1, HD),
        left[:, :, :, 1].reshape(-1, HD),
    )


def body(span_q, span_k, span_v, q_gain, k_gain, kv_cache, frame_home, chosen_frames):
    rows = span_q.shape[0]
    share = rows // GROUP
    v_main = to_heads(span_v[:, :MAIN])
    v_left = lax.all_to_all(span_v[:, MAIN:], "h", 0, 1, tiled=True)
    query_float = span_q.astype(jnp.float32)
    key_float = span_k.astype(jnp.float32)
    squares = jnp.stack(
        [jnp.sum(query_float * query_float, axis=-1), jnp.sum(key_float * key_float, axis=-1)]
    )
    squares = lax.psum(squares, "h")
    inverse = lax.rsqrt(squares / D + 1e-06)
    keys = (key_float * inverse[1][:, None] * k_gain).astype(jnp.bfloat16)
    queries = (query_float * inverse[0][:, None] * q_gain).astype(jnp.bfloat16)
    k_left = lax.all_to_all(keys[:, MAIN:], "h", 0, 1, tiled=True)
    q_left = lax.all_to_all(queries[:, MAIN:], "h", 0, 1, tiled=True)
    kv = to_heads(jnp.concatenate([keys[:, :MAIN], k_left, v_left], axis=0))
    kv = kv.reshape(ZED, rows + 2 * share, HD)
    k_main = kv[:, :rows].reshape(-1, HD)
    left = lax.all_gather(kv[:, rows:], "h", axis=0)
    k_rest = left[:, :, :share].reshape(-1, HD)
    v_rest = left[:, :, share:].reshape(-1, HD)
    kc_main, vc_main, kc_rest, vc_rest = cached_frames(kv_cache, frame_home[chosen_frames])

    main_side = (k_main, with_ones(v_main), kc_main, with_ones(vc_main))
    rest_side = (k_rest, with_ones(v_rest), kc_rest, with_ones(vc_rest))
    main_out = []
    for kind, first, count in PARTS:
        source = queries[:, :MAIN] if kind == "m" else q_left
        q = to_heads(source[first : first + count])
        out = attend(q, *(main_side if kind == "m" else rest_side))
        out = lax.all_to_all(out, "z", 0, 1, tiled=True)
        if kind == "m":
            main_out.append(out)
        else:
            rest_out = lax.all_to_all(out, "h", 1, 0, tiled=True)
    return jnp.concatenate([jnp.concatenate(main_out, axis=0), rest_out], axis=1)


def solution(mesh):
    grid = Mesh(mesh.devices.reshape(CAND, ZED, GROUP), ("cand", "z", "h"))
    tokens = P(("cand", "z"), "h")
    placed = (
        tokens,
        tokens,
        tokens,
        P("h"),
        P("h"),
        P(("cand", "z"), None, None, "h"),
        P(),
        P(),
    )
    return jax.shard_map(body, mesh=grid, in_specs=placed, out_specs=tokens, check_vma=False)
```

```python
import functools
import math

import jax
import jax.numpy as jnp
from jax import lax
from jax.experimental import pallas as pl
from jax.experimental.pallas import tpu as pltpu
from jax.sharding import Mesh, PartitionSpec as P

D = 5120
HD = 128
FT = 128
SEL = 5
CAND = 8
ZED = 8
GROUP = 4
MAIN = ZED * HD
REST = 2 * HD
CAP = 30.0
LOG2E = math.log2(math.e)
ORDER = (1, 7, 4, 2, 6, 3, 5)
KEY_BLOCK = 512


def add_keys(q, k, v, total):
    scores = lax.dot_general(q, k, (((1,), (1,)), ((), ())), preferred_element_type=jnp.float32)
    capped = jnp.tanh(scores * (1.0 / (CAP * math.sqrt(HD))))
    weights = jnp.exp2(capped * (CAP * LOG2E) - CAP * LOG2E).astype(jnp.bfloat16)
    v = jnp.concatenate([v, jnp.ones_like(v)], axis=1)
    term = jnp.dot(weights, v, preferred_element_type=jnp.float32)
    return term if total is None else total + term


def add_range(q, k_ref, v_ref, total):
    count = k_ref.shape[0]
    for first in range(0, count, KEY_BLOCK):
        part = pl.ds(first, min(KEY_BLOCK, count - first))
        total = add_keys(q, k_ref[part, :], v_ref[part, :], total)
    return total


def quotient(total):
    return (total[:, :HD] / total[:, HD:]).astype(jnp.bfloat16)


def main_kernel(z_ref, q_ref, k_ref, *refs):
    values, (kc_ref, vc_ref, o_ref) = refs[:ZED], refs[ZED:]
    q = q_ref[...]
    total = None
    for shift, v_ref in enumerate(values):
        source = lax.rem(z_ref[0] + (ZED - shift), ZED)
        total = add_keys(q, k_ref[source, : v_ref.shape[0], :], v_ref[...], total)
    o_ref[...] = quotient(add_range(q, kc_ref, vc_ref, total))


def rest_kernel(q_ref, k_ref, v_ref, kc_ref, vc_ref, o_ref):
    q = q_ref[...]
    total = add_range(q, k_ref, v_ref, None)
    o_ref[...] = quotient(add_range(q, kc_ref, vc_ref, total))


def cost(rows, keys):
    return pl.CostEstimate(
        flops=2 * rows * keys * 4 * HD * 2,
        bytes_accessed=2 * (2 * rows + 2 * keys) * HD,
        transcendentals=2 * rows * keys,
    )


def attend_main(z, q, k, values, kc, vc):
    whole = pl.BlockSpec(memory_space=pltpu.VMEM)
    return pl.pallas_call(
        main_kernel,
        in_specs=[pl.BlockSpec(memory_space=pltpu.SMEM)] + [whole] * (len(values) + 4),
        out_specs=whole,
        out_shape=jax.ShapeDtypeStruct(q.shape, jnp.bfloat16),
        compiler_params=pltpu.CompilerParams(vmem_limit_bytes=24 * 2**20),
        cost_estimate=cost(q.shape[0], ZED * 512 + SEL * FT),
    )(z, q, k, *values, kc, vc)


def attend_rest(q, k, v, kc, vc, block=512):
    whole = pl.BlockSpec(memory_space=pltpu.VMEM)
    rows = pl.BlockSpec((block, HD), lambda i: (i, 0))
    return pl.pallas_call(
        rest_kernel,
        grid=(q.shape[0] // block,),
        in_specs=[rows, whole, whole, whole, whole],
        out_specs=rows,
        out_shape=jax.ShapeDtypeStruct(q.shape, jnp.bfloat16),
        compiler_params=pltpu.CompilerParams(vmem_limit_bytes=24 * 2**20),
        cost_estimate=cost(q.shape[0], k.shape[0] + kc.shape[0]),
    )(q, k, v, kc, vc)


def shifted(x, shift):
    return lax.ppermute(x, "z", [(i, (i + shift) % ZED) for i in range(ZED)])


def swapped(x, axis, bits):
    return lax.ppermute(x, axis, [(i, i ^ bits) for i in range(lax.axis_size(axis))])


def exchanged(x, axis):
    return lax.all_to_all(x, axis, 0, 0, tiled=True)


def after(x, values, shifts):
    tied = lax.optimization_barrier((x, *[values[d] for d in shifts]))
    for d, value in zip(shifts, tied[1:]):
        values[d] = value
    return tied[0]


def head_of(x, index):
    return lax.dynamic_slice_in_dim(x, index * HD, HD, 1)


def body(span_q, span_k, span_v, q_gain, k_gain, kv_cache, frame_home, chosen_frames):
    rows = span_q.shape[0]
    share = rows // GROUP
    z, h = lax.axis_index("z"), lax.axis_index("h")
    locations = frame_home[chosen_frames]

    values = {0: head_of(span_v, z)}
    for d in ORDER:
        values[d] = shifted(head_of(span_v, (z + d) % ZED), d)

    cache_rest = kv_cache[..., MAIN:].reshape(2, 2, GROUP, FT // GROUP, REST)
    cache_rest = cache_rest.transpose(2, 0, 1, 3, 4).reshape(GROUP, 2 * 2 * FT // GROUP, REST)
    rest = [x[:, MAIN:].reshape(GROUP, share, REST) for x in (span_q, span_k, span_v)]
    rest = exchanged(jnp.concatenate(rest + [cache_rest], axis=2), "h")
    q_rest, k_rest, v_rest, c_rest = [rest[:, :, i * REST : (i + 1) * REST] for i in range(4)]
    q_rest, k_rest, v_rest = [x.transpose(1, 0, 2).reshape(share, MAIN) for x in (q_rest, k_rest, v_rest)]

    query_float = span_q.astype(jnp.float32)
    key_float = span_k.astype(jnp.float32)
    sums = jnp.stack([jnp.sum(query_float * query_float, axis=-1), jnp.sum(key_float * key_float, axis=-1)])
    gains = jnp.stack([q_gain[MAIN:], k_gain[MAIN:]])
    gains = jnp.where((jnp.arange(GROUP) == h)[None, :, None], gains[:, None, :], 0.0)
    both = lax.psum(jnp.concatenate([sums, gains.reshape(2, GROUP * REST)], axis=1), "h")
    inverse = lax.rsqrt(both[:, :rows] / D + 1e-06)
    inverse_share = lax.dynamic_slice_in_dim(inverse, h * share, share, 1)
    gains = both[:, rows:]

    def normed(x, which, factor, gain):
        return (x.astype(jnp.float32) * factor[which][:, None] * gain).astype(jnp.bfloat16)

    keys = normed(span_k[:, :MAIN], 1, inverse, k_gain[:MAIN])
    queries = normed(span_q[:, :MAIN], 0, inverse, q_gain[:MAIN])
    k_rest = normed(k_rest, 1, inverse_share, gains[1])
    q_rest = normed(q_rest, 0, inverse_share, gains[0])

    part = FT // CAND
    small = part // GROUP
    frames = kv_cache[..., :MAIN].reshape(2, 2, CAND, part, MAIN).transpose(2, 0, 1, 3, 4)
    c_rest = c_rest.reshape(GROUP, 2, 2, CAND, small, REST).transpose(3, 1, 2, 4, 0, 5)
    c_rest = c_rest.reshape(CAND, 2, 2, small, MAIN)
    frames = jnp.concatenate([frames, c_rest], axis=3).reshape(CAND, 4 * (part + small), MAIN)
    frames = exchanged(after(frames, values, ORDER[:2]), "cand").reshape(2 * CAND, 2 * (part + small), MAIN)
    home = locations // 2
    slot = (home // ZED) * 2 + locations % 2
    chosen = jnp.concatenate(
        [lax.dynamic_index_in_dim(frames, slot[s], 0, keepdims=False) for s in range(SEL)], axis=0
    )
    chosen = jnp.stack([chosen[:, i * HD : (i + 1) * HD] for i in range(ZED)])
    chosen = exchanged(after(chosen, values, ORDER[2:5]), "z").reshape(ZED, SEL, 2 * (part + small), HD)
    chosen = jnp.stack(
        [lax.dynamic_index_in_dim(chosen[:, s], home[s] % ZED, 0, keepdims=False) for s in range(SEL)]
    )
    every = jnp.stack([chosen] + [swapped(chosen, "cand", bits) for bits in range(1, CAND)])
    every = every.reshape(CAND, SEL, 2, part + small, HD)
    kc, vc = [every[:, :, i, :part].reshape(-1, HD) for i in range(2)]
    cached_rest = every[:, :, :, part:].reshape(CAND, SEL * 2 * small, HD)

    kv = jnp.concatenate([keys, k_rest, v_rest], axis=0)
    kv = lax.all_to_all(after(kv, values, ORDER[5:]), "z", 1, 0, tiled=True).reshape(ZED, rows + 2 * share, HD)

    values = [values[d] for d in range(ZED)]

    q_rest, kv = lax.optimization_barrier((q_rest, kv))
    q_rest = lax.all_to_all(q_rest, "z", 1, 0, tiled=True)
    together = jnp.concatenate([kv[:, rows:], cached_rest], axis=1)[None]
    together = jnp.concatenate([together, swapped(together, "h", 2)], axis=0)
    together = jnp.concatenate([together, swapped(together, "h", 1)], axis=0)
    cached_rest = together[:, :, 2 * share :].reshape(GROUP, CAND, SEL, 2, small, HD)
    out_rest = attend_rest(
        q_rest,
        together[:, :, :share].reshape(-1, HD),
        together[:, :, share : 2 * share].reshape(-1, HD),
        cached_rest[:, :, :, 0].reshape(-1, HD),
        cached_rest[:, :, :, 1].reshape(-1, HD),
    )
    out_rest = exchanged(out_rest.reshape(ZED, share, HD), "z")
    out_rest = out_rest.reshape(GROUP, 2, share, HD).transpose(0, 2, 1, 3).reshape(GROUP, share, REST)
    out_rest = exchanged(out_rest, "h").reshape(rows, REST)

    where = z.astype(jnp.int32).reshape(1)
    out = jnp.zeros((rows, MAIN), jnp.bfloat16)
    for d in (0,) + ORDER:
        q = head_of(queries, (z + d) % ZED)
        if d:
            q = shifted(q, d)
        o = attend_main(where, q, kv, values, kc, vc)
        if d:
            o = shifted(o, ZED - d)
        out = lax.dynamic_update_slice_in_dim(out, o, ((z + d) % ZED) * HD, 1)
    return jnp.concatenate([out, out_rest], axis=1)


def solution(mesh):
    grid = Mesh(mesh.devices.reshape(CAND, ZED, GROUP), ("cand", "z", "h"))
    tokens = P(("cand", "z"), "h")
    placed = (
        tokens,
        tokens,
        tokens,
        P("h"),
        P("h"),
        P(("cand", "z"), None, None, "h"),
        P(),
        P(),
    )
    return jax.shard_map(body, mesh=grid, in_specs=placed, out_specs=tokens, check_vma=False)
```

```python
import functools
import math

import jax
import jax.numpy as jnp
from jax import lax
from jax.experimental import pallas as pl
from jax.experimental.pallas import tpu as pltpu
from jax.sharding import Mesh, PartitionSpec as P

D = 5120
HD = 128
FT = 128
SEL = 5
CAND = 8
ZED = 8
GROUP = 4
MAIN = ZED * HD
REST = 2 * HD
CAP = 30.0
LOG2E = math.log2(math.e)
ORDER = (1, 7, 4, 2, 6, 3, 5)
KEY_BLOCK = 512
PART = FT // CAND
PICKED = SEL * PART
EACH = 3

VMEM = pl.BlockSpec(memory_space=pltpu.VMEM)
SMEM = pl.BlockSpec(memory_space=pltpu.SMEM)


def is_shape(x):
    return isinstance(x[0], int)


def kernel_call(kernel, shape, scalars, arrays, cost=None):
    return pl.pallas_call(
        kernel,
        in_specs=[SMEM] * len(scalars) + [VMEM] * len(arrays),
        out_specs=VMEM if is_shape(shape) else [VMEM] * len(shape),
        out_shape=jax.tree.map(lambda x: jax.ShapeDtypeStruct(x, jnp.bfloat16), shape, is_leaf=is_shape),
        compiler_params=pltpu.CompilerParams(vmem_limit_bytes=24 * 2**20),
        cost_estimate=cost,
    )(*scalars, *arrays)


def add_keys(q, k, v, total):
    scores = lax.dot_general(q, k, (((1,), (1,)), ((), ())), preferred_element_type=jnp.float32)
    capped = jnp.tanh(scores * (1.0 / (CAP * math.sqrt(HD))))
    weights = jnp.exp2(capped * (CAP * LOG2E) - CAP * LOG2E).astype(jnp.bfloat16)
    v = jnp.concatenate([v, jnp.ones_like(v)], axis=1)
    term = jnp.dot(weights, v, preferred_element_type=jnp.float32)
    return term if total is None else total + term


def add_cached(q, k, v, total):
    for first in range(0, SEL * FT, KEY_BLOCK):
        part = slice(first, min(first + KEY_BLOCK, SEL * FT))
        total = add_keys(q, k[part], v[part], total)
    return total


def quotient(total):
    return (total[:, :HD] / total[:, HD:]).astype(jnp.bfloat16)


def main_kernel(z_ref, q_ref, k_ref, *refs):
    values, cached, o_ref = refs[:ZED], refs[ZED : ZED + CAND], refs[-1]
    q = q_ref[...]
    total = None
    for shift, v_ref in enumerate(values):
        source = lax.rem(z_ref[0] + (ZED - shift), ZED)
        total = add_keys(q, k_ref[source, : v_ref.shape[0], :], v_ref[...], total)
    kc = jnp.concatenate([ref[:PICKED, :] for ref in cached], axis=0)
    vc = jnp.concatenate([ref[PICKED : 2 * PICKED, :] for ref in cached], axis=0)
    o_ref[...] = quotient(add_cached(q, kc, vc, total))


def rest_kernel(share, entry_ref, q_ref, all_ref, o_ref):
    per = KEY_BLOCK // share

    @pl.loop(0, q_ref.shape[0] // KEY_BLOCK)
    def _(step):
        rows = pl.ds(pl.multiple_of(step * KEY_BLOCK, KEY_BLOCK), KEY_BLOCK)
        q = q_ref[rows, :]
        total = None
        for first in range(0, all_ref.shape[0], per):
            k = all_ref[first : first + per, :share, :].reshape(KEY_BLOCK, HD)
            v = all_ref[first : first + per, share : 2 * share, :].reshape(KEY_BLOCK, HD)
            total = add_keys(q, k, v, total)
        blocks = []
        for b in range(2 * SEL):
            at = pl.ds(entry_ref[b // EACH] * CAND, CAND)
            first = 2 * share + (b % EACH) * PART
            blocks.append(all_ref[at, first : first + PART, :].reshape(FT, HD))
        kc = jnp.concatenate(blocks[:SEL], axis=0)
        vc = jnp.concatenate(blocks[SEL:], axis=0)
        o_ref[rows, :] = quotient(add_cached(q, kc, vc, total))


def choose_kernel(cand_ref, slot_ref, frames_ref, main_ref, rest_ref):
    rest_ref[...] = jnp.zeros_like(rest_ref)
    for s in range(SEL):
        for kind in range(2):
            b = kind * SEL + s
            block = frames_ref[cand_ref[s] * 4 + slot_ref[s] * 2 + kind]
            for j in range(ZED):
                main_ref[j, b * PART : (b + 1) * PART, :] = block[:, j * HD : (j + 1) * HD]
            rest_ref[b // EACH, (b % EACH) * PART : (b % EACH + 1) * PART, :] = block[:, MAIN:]


def append_kernel(main_ref, rest_ref, o_ref):
    count = main_ref.shape[1]
    for j in range(ZED):
        o_ref[j, :count, :] = main_ref[j]
        o_ref[j, count:, :] = rest_ref[j // 2, -EACH * PART :, (j % 2) * HD : (j % 2 + 1) * HD]


def take_kernel(source_ref, from_ref, o_ref):
    for b in range(2 * SEL + EACH):
        o_ref[b * PART : (b + 1) * PART, :] = from_ref[source_ref[b], b * PART : (b + 1) * PART, :]


def normed(x, inverse, gain):
    return (x.astype(jnp.float32) * inverse * gain).astype(jnp.bfloat16)


def pack_kernel(share, k_ref, rest_ref, inverse_ref, inverse_share_ref, gain_ref, rest_gain_ref, o_ref):
    rows = k_ref.shape[0]
    for j in range(ZED):
        column = slice(j * HD, (j + 1) * HD)
        o_ref[j, :rows, :] = normed(k_ref[:, column], inverse_ref[1], gain_ref[:, column])
        g, column = j // 2, slice((j % 2) * HD, (j % 2 + 1) * HD)
        for place, which in ((0, 1), (2, 0)):
            x = rest_ref[g, which * share : (which + 1) * share, column]
            gain = rest_gain_ref[which * GROUP + g : which * GROUP + g + 1, column]
            first = rows + place * share
            o_ref[j, first : first + share, :] = normed(x, inverse_share_ref[which], gain)
        o_ref[j, rows + share : rows + 2 * share, :] = rest_ref[g, 2 * share : 3 * share, column]


def query_kernel(z_ref, q_ref, inverse_ref, gain_ref, o_ref):
    for j in range(ZED):
        column = slice(j * HD, (j + 1) * HD)
        shift = lax.rem(j + ZED - z_ref[0], ZED)
        o_ref[shift] = normed(q_ref[:, column], inverse_ref[0], gain_ref[:, column])


def join_kernel(z_ref, *refs):
    outs, rest_ref, o_ref = refs[:ZED], refs[ZED], refs[-1]
    for shift, ref in enumerate(outs):
        column = pl.multiple_of(lax.rem(z_ref[0] + shift, ZED) * HD, HD)
        o_ref[:, pl.ds(column, HD)] = ref[...]
    share = rest_ref.shape[1]
    for i in range(GROUP):
        o_ref[i * share : (i + 1) * share, MAIN:] = rest_ref[i]


def cost(rows, keys):
    return pl.CostEstimate(
        flops=2 * rows * keys * 4 * HD * 2,
        bytes_accessed=2 * (2 * rows + 2 * keys) * HD,
        transcendentals=2 * rows * keys,
    )


def shifted(x, shift):
    return lax.ppermute(x, "z", [(i, (i + shift) % ZED) for i in range(ZED)])


def swapped(x, axis, bits):
    return lax.ppermute(x, axis, [(i, i ^ bits) for i in range(lax.axis_size(axis))])


def exchanged(x, axis):
    return lax.all_to_all(x, axis, 0, 0, tiled=True)


def after(x, values, shifts):
    tied = lax.optimization_barrier((x, *[values[d] for d in shifts]))
    for d, value in zip(shifts, tied[1:]):
        values[d] = value
    return tied[0]


def head_of(x, index):
    return lax.dynamic_slice_in_dim(x, index * HD, HD, 1)


def body(span_q, span_k, span_v, q_gain, k_gain, kv_cache, frame_home, chosen_frames):
    rows = span_q.shape[0]
    share = rows // GROUP
    z, h = lax.axis_index("z"), lax.axis_index("h")
    where = z.astype(jnp.int32).reshape(1)

    locations = frame_home[chosen_frames]
    home, slot = locations // 2, locations % 2
    cand, keeper = home // ZED, home % ZED
    own = (EACH * h + jnp.arange(EACH)) % SEL
    own = jnp.sum(jnp.where(own[:, None] == jnp.arange(SEL)[None, :], keeper[None, :], 0), axis=1)
    keeper = jnp.concatenate([keeper, keeper, own]).astype(jnp.int32)
    entry = jnp.arange(GROUP, dtype=jnp.int32) ^ h
    entry = (entry % 2) * 2 + entry // 2

    frames = kv_cache.reshape(4, CAND, PART, MAIN + REST).transpose(1, 0, 2, 3)
    frames = exchanged(frames, "cand").reshape(CAND * 4, PART, MAIN + REST)
    chosen, c_rest = kernel_call(
        choose_kernel,
        ((ZED, 2 * PICKED, HD), (GROUP, EACH * PART, REST)),
        (cand, slot),
        (frames,),
    )

    values = {0: head_of(span_v, z)}
    for d in ORDER:
        values[d] = shifted(head_of(span_v, (z + d) % ZED), d)

    rest = [x[:, MAIN:].reshape(GROUP, share, REST) for x in (span_q, span_k, span_v)]
    rest = jnp.concatenate(rest + [c_rest], axis=1)
    rest = exchanged(after(rest, values, ORDER[:2]), "h")

    query_float = span_q.astype(jnp.float32)
    key_float = span_k.astype(jnp.float32)
    sums = jnp.stack([jnp.sum(query_float * query_float, axis=-1), jnp.sum(key_float * key_float, axis=-1)])
    gains = jnp.stack([q_gain[MAIN:], k_gain[MAIN:]])
    gains = jnp.where((jnp.arange(GROUP) == h)[None, :, None], gains[:, None, :], 0.0)
    both = lax.psum(jnp.concatenate([sums, gains.reshape(2, GROUP * REST)], axis=1), "h")
    inverse = lax.rsqrt(both[:, :rows] / D + 1e-06)
    inverse_share = lax.dynamic_slice_in_dim(inverse, h * share, share, 1)
    inverse = jnp.broadcast_to(inverse[:, :, None], (2, rows, HD))
    inverse_share = jnp.broadcast_to(inverse_share[:, :, None], (2, share, HD))
    gains = both[:, rows:].reshape(2 * GROUP, REST)

    chosen = kernel_call(append_kernel, (ZED, 2 * PICKED + EACH * PART, HD), (), (chosen, rest))
    chosen = exchanged(after(chosen, values, ORDER[2:5]), "z")

    kv = kernel_call(
        functools.partial(pack_kernel, share),
        (ZED, rows + 3 * share, HD),
        (),
        (span_k, rest, inverse, inverse_share, k_gain.reshape(1, -1), gains),
    )
    kv, chosen = lax.optimization_barrier((kv, chosen))
    kv = exchanged(after(kv, values, ORDER[5:]), "z")
    values = [values[d] for d in range(ZED)]

    chosen = kernel_call(take_kernel, (2 * PICKED + EACH * PART, HD), (keeper,), (chosen,))
    cached = [chosen] + [swapped(chosen, "cand", bits) for bits in range(1, CAND)]

    queries = kernel_call(
        query_kernel, (ZED, rows, HD), (where,), (span_q, inverse, q_gain.reshape(1, -1))
    )
    queries, *cached = lax.optimization_barrier((queries, *cached))

    together = jnp.stack([x[2 * PICKED :] for x in cached])
    together = jnp.concatenate([kv[:, rows : rows + 2 * share], together], axis=1)
    together = jnp.concatenate([together, swapped(together, "h", 2)], axis=0)
    together = jnp.concatenate([together, swapped(together, "h", 1)], axis=0)
    out_rest = kernel_call(
        functools.partial(rest_kernel, share),
        (ZED * share, HD),
        (entry,),
        (kv[:, rows + 2 * share :].reshape(ZED * share, HD), together),
        cost(ZED * share, ZED * rows + SEL * FT),
    )

    outs = {}
    for i, d in enumerate((0,) + ORDER):
        q = queries[d]
        if d:
            q = shifted(q, d)
        if i == 4:
            q, out_rest = lax.optimization_barrier((q, out_rest))
        o = kernel_call(
            main_kernel, (rows, HD), (where,), (q, kv, *values, *cached), cost(rows, ZED * rows + SEL * FT)
        )
        outs[d] = shifted(o, ZED - d) if d else o

    out_rest = exchanged(out_rest.reshape(ZED, share, HD), "z")
    out_rest = jnp.concatenate([out_rest[0::2], out_rest[1::2]], axis=2)
    out_rest = exchanged(out_rest, "h")
    return kernel_call(
        join_kernel, (rows, MAIN + REST), (where,), [outs[d] for d in range(ZED)] + [out_rest]
    )


def solution(mesh):
    grid = Mesh(mesh.devices.reshape(CAND, ZED, GROUP), ("cand", "z", "h"))
    tokens = P(("cand", "z"), "h")
    placed = (
        tokens,
        tokens,
        tokens,
        P("h"),
        P("h"),
        P(("cand", "z"), None, None, "h"),
        P(),
        P(),
    )
    return jax.shard_map(body, mesh=grid, in_specs=placed, out_specs=tokens, check_vma=False)
```

```python
import functools
import math

import jax
import jax.numpy as jnp
from jax import lax
from jax.experimental import pallas as pl
from jax.experimental.pallas import tpu as pltpu
from jax.sharding import Mesh, PartitionSpec as P

D = 5120
HD = 128
FT = 128
SEL = 5
CAND = 8
ZED = 8
GROUP = 4
MAIN = ZED * HD
REST = 2 * HD
CAP = 30.0
LOG2E = math.log2(math.e)
ORDER = (1, 7, 4, 2, 6, 3, 5)
SEND = (4, 3, 5, 2, 6, 1, 7, 0)
KEY_BLOCK = 512
PART = FT // CAND
PICKED = SEL * PART
EACH = 3

VMEM = pl.BlockSpec(memory_space=pltpu.VMEM)
SMEM = pl.BlockSpec(memory_space=pltpu.SMEM)


def is_shape(x):
    return isinstance(x[0], int)


def kernel_call(kernel, shape, scalars, arrays, cost=None):
    return pl.pallas_call(
        kernel,
        in_specs=[SMEM] * len(scalars) + [VMEM] * len(arrays),
        out_specs=VMEM if is_shape(shape) else [VMEM] * len(shape),
        out_shape=jax.tree.map(lambda x: jax.ShapeDtypeStruct(x, jnp.bfloat16), shape, is_leaf=is_shape),
        compiler_params=pltpu.CompilerParams(vmem_limit_bytes=28 * 2**20),
        cost_estimate=cost,
    )(*scalars, *arrays)


def add_keys(q, k, v, total):
    scores = lax.dot_general(q, k, (((1,), (1,)), ((), ())), preferred_element_type=jnp.float32)
    capped = jnp.tanh(scores * (1.0 / (CAP * math.sqrt(HD))))
    weights = jnp.exp2(capped * (CAP * LOG2E) - CAP * LOG2E).astype(jnp.bfloat16)
    v = jnp.concatenate([v, jnp.ones_like(v)], axis=1)
    term = jnp.dot(weights, v, preferred_element_type=jnp.float32)
    return term if total is None else total + term


def add_cached(q, k, v, total):
    for first in range(0, SEL * FT, KEY_BLOCK):
        part = slice(first, min(first + KEY_BLOCK, SEL * FT))
        total = add_keys(q, k[part], v[part], total)
    return total


def quotient(total):
    return (total[:, :HD] / total[:, HD:]).astype(jnp.bfloat16)


def main_kernel(q_ref, k_ref, v_ref, cached_ref, o_ref):
    q = q_ref[...]
    total = None
    for first in range(0, k_ref.shape[0], KEY_BLOCK):
        part = pl.ds(first, KEY_BLOCK)
        total = add_keys(q, k_ref[part, :], v_ref[part, :], total)
    kc = cached_ref[:, :PICKED, :].reshape(SEL * FT, HD)
    vc = cached_ref[:, PICKED : 2 * PICKED, :].reshape(SEL * FT, HD)
    o_ref[...] = quotient(add_cached(q, kc, vc, total))


def split_kernel(z_ref, kq_ref, *refs):
    pieces, (k_ref, v_ref, q_ref) = refs[:ZED], refs[ZED:]
    rows = pieces[0].shape[0]
    for shift, piece in enumerate(pieces):
        v_ref[shift * rows : (shift + 1) * rows, :] = piece[...]
        source = lax.rem(z_ref[0] + (ZED - shift), ZED)
        k_ref[shift * rows : (shift + 1) * rows, :] = kq_ref[source, :rows, :]
        q_ref[shift] = kq_ref[source, rows:, :]


def rest_kernel(share, entry_ref, q_ref, all_ref, o_ref):
    per = KEY_BLOCK // share

    @pl.loop(0, q_ref.shape[0] // KEY_BLOCK)
    def _(step):
        rows = pl.ds(pl.multiple_of(step * KEY_BLOCK, KEY_BLOCK), KEY_BLOCK)
        q = q_ref[rows, :]
        total = None
        for first in range(0, all_ref.shape[0], per):
            k = all_ref[first : first + per, :share, :].reshape(KEY_BLOCK, HD)
            v = all_ref[first : first + per, share : 2 * share, :].reshape(KEY_BLOCK, HD)
            total = add_keys(q, k, v, total)
        blocks = []
        for b in range(2 * SEL):
            at = pl.ds(entry_ref[b // EACH] * CAND, CAND)
            first = 2 * share + (b % EACH) * PART
            blocks.append(all_ref[at, first : first + PART, :].reshape(FT, HD))
        kc = jnp.concatenate(blocks[:SEL], axis=0)
        vc = jnp.concatenate(blocks[SEL:], axis=0)
        o_ref[rows, :] = quotient(add_cached(q, kc, vc, total))


def choose_kernel(cand_ref, slot_ref, frames_ref, main_ref, rest_ref):
    rest_ref[...] = jnp.zeros_like(rest_ref)
    for s in range(SEL):
        for kind in range(2):
            b = kind * SEL + s
            block = frames_ref[cand_ref[s] * 4 + slot_ref[s] * 2 + kind]
            for j in range(ZED):
                main_ref[j, b * PART : (b + 1) * PART, :] = block[:, j * HD : (j + 1) * HD]
            rest_ref[b // EACH, (b % EACH) * PART : (b % EACH + 1) * PART, :] = block[:, MAIN:]


def append_kernel(main_ref, rest_ref, o_ref):
    count = main_ref.shape[1]
    for j in range(ZED):
        o_ref[j, :count, :] = main_ref[j]
        o_ref[j, count:, :] = rest_ref[j // 2, -EACH * PART :, (j % 2) * HD : (j % 2 + 1) * HD]


def take_kernel(source_ref, from_ref, o_ref):
    for b in range(2 * SEL + EACH):
        o_ref[b * PART : (b + 1) * PART, :] = from_ref[source_ref[b], b * PART : (b + 1) * PART, :]


def normed(x, inverse, gain):
    return (x.astype(jnp.float32) * inverse * gain).astype(jnp.bfloat16)


def pack_kernel(share, q_in_ref, k_ref, rest_ref, inverse_ref, inverse_share_ref, q_gain_ref, gain_ref, rest_gain_ref, o_ref, left_ref):
    rows = k_ref.shape[0]
    for j in range(ZED):
        column = slice(j * HD, (j + 1) * HD)
        o_ref[j, :rows, :] = normed(k_ref[:, column], inverse_ref[1], gain_ref[:, column])
        g, column = j // 2, slice((j % 2) * HD, (j % 2 + 1) * HD)
        for place, which in ((0, 1), (2, 0)):
            x = rest_ref[g, which * share : (which + 1) * share, column]
            gain = rest_gain_ref[which * GROUP + g : which * GROUP + g + 1, column]
            first = place * share
            left_ref[j, first : first + share, :] = normed(x, inverse_share_ref[which], gain)
        main = slice(j * HD, (j + 1) * HD)
        o_ref[j, rows:, :] = normed(q_in_ref[:, main], inverse_ref[0], q_gain_ref[:, main])
        left_ref[j, share : 2 * share, :] = rest_ref[g, 2 * share : 3 * share, column]


def join_kernel(z_ref, *refs):
    outs, rest_ref, o_ref = refs[:ZED], refs[ZED], refs[-1]
    for shift, ref in enumerate(outs):
        column = pl.multiple_of(lax.rem(z_ref[0] + shift, ZED) * HD, HD)
        o_ref[:, pl.ds(column, HD)] = ref[...]
    share = rest_ref.shape[1]
    for i in range(GROUP):
        o_ref[i * share : (i + 1) * share, MAIN:] = rest_ref[i]


def cost(rows, keys):
    return pl.CostEstimate(
        flops=2 * rows * keys * 4 * HD * 2,
        bytes_accessed=2 * (2 * rows + 2 * keys) * HD,
        transcendentals=2 * rows * keys,
    )


def shifted(x, shift):
    return lax.ppermute(x, "z", [(i, (i + shift) % ZED) for i in range(ZED)])


def swapped(x, axis, bits):
    return lax.ppermute(x, axis, [(i, i ^ bits) for i in range(lax.axis_size(axis))])


def exchanged(x, axis):
    return lax.all_to_all(x, axis, 0, 0, tiled=True)


def after(x, values, shifts):
    tied = lax.optimization_barrier((x, *[values[d] for d in shifts]))
    for d, value in zip(shifts, tied[1:]):
        values[d] = value
    return tied[0]


def head_of(x, index):
    return lax.dynamic_slice_in_dim(x, index * HD, HD, 1)


def body(span_q, span_k, span_v, q_gain, k_gain, kv_cache, frame_home, chosen_frames):
    rows = span_q.shape[0]
    share = rows // GROUP
    z, h = lax.axis_index("z"), lax.axis_index("h")
    where = z.astype(jnp.int32).reshape(1)

    locations = frame_home[chosen_frames]
    home, slot = locations // 2, locations % 2
    cand, keeper = home // ZED, home % ZED
    own = (EACH * h + jnp.arange(EACH)) % SEL
    own = jnp.sum(jnp.where(own[:, None] == jnp.arange(SEL)[None, :], keeper[None, :], 0), axis=1)
    keeper = jnp.concatenate([keeper, keeper, own]).astype(jnp.int32)
    entry = jnp.arange(GROUP, dtype=jnp.int32) ^ h
    entry = (entry % 2) * 2 + entry // 2

    frames = kv_cache.reshape(4, CAND, PART, MAIN + REST).transpose(1, 0, 2, 3)
    frames = exchanged(frames, "cand").reshape(CAND * 4, PART, MAIN + REST)
    chosen, c_rest = kernel_call(
        choose_kernel,
        ((ZED, 2 * PICKED, HD), (GROUP, EACH * PART, REST)),
        (cand, slot),
        (frames,),
    )

    values = {0: head_of(span_v, z)}
    for d in ORDER:
        values[d] = shifted(head_of(span_v, (z + d) % ZED), d)

    rest = [x[:, MAIN:].reshape(GROUP, share, REST) for x in (span_q, span_k, span_v)]
    rest = jnp.concatenate(rest + [c_rest], axis=1)
    rest = exchanged(after(rest, values, ORDER[:2]), "h")

    query_float = span_q.astype(jnp.float32)
    key_float = span_k.astype(jnp.float32)
    sums = jnp.stack([jnp.sum(query_float * query_float, axis=-1), jnp.sum(key_float * key_float, axis=-1)])
    gains = jnp.stack([q_gain[MAIN:], k_gain[MAIN:]])
    gains = jnp.where((jnp.arange(GROUP) == h)[None, :, None], gains[:, None, :], 0.0)
    both = lax.psum(jnp.concatenate([sums, gains.reshape(2, GROUP * REST)], axis=1), "h")
    inverse = lax.rsqrt(both[:, :rows] / D + 1e-06)
    inverse_share = lax.dynamic_slice_in_dim(inverse, h * share, share, 1)
    inverse = jnp.broadcast_to(inverse[:, :, None], (2, rows, HD))
    inverse_share = jnp.broadcast_to(inverse_share[:, :, None], (2, share, HD))
    gains = both[:, rows:].reshape(2 * GROUP, REST)

    chosen = kernel_call(append_kernel, (ZED, 2 * PICKED + EACH * PART, HD), (), (chosen, rest))
    chosen = exchanged(after(chosen, values, ORDER[2:5]), "z")

    keys, left = kernel_call(
        functools.partial(pack_kernel, share),
        ((ZED, 2 * rows, HD), (ZED, 3 * share, HD)),
        (),
        (span_q, span_k, rest, inverse, inverse_share, q_gain.reshape(1, -1), k_gain.reshape(1, -1), gains),
    )
    left, chosen = lax.optimization_barrier((left, chosen))
    left = exchanged(left, "z")

    chosen = kernel_call(take_kernel, (2 * PICKED + EACH * PART, HD), (keeper,), (chosen,))
    cached = chosen[None]
    for bits in (1, 2, 4):
        cached = jnp.concatenate([cached, swapped(cached, "cand", bits)], axis=0)

    keys, left, cached = lax.optimization_barrier((keys, left, cached))
    keys = exchanged(after(keys, values, ORDER[5:]), "z")
    values = [values[d] for d in range(ZED)]

    together = jnp.concatenate([left[:, : 2 * share], cached[:, 2 * PICKED :]], axis=1)
    for bits in (2, 1):
        together = jnp.concatenate([together, swapped(together, "h", bits)], axis=0)
    out_rest = kernel_call(
        functools.partial(rest_kernel, share),
        (ZED * share, HD),
        (entry,),
        (left[:, 2 * share :].reshape(ZED * share, HD), together),
        cost(ZED * share, ZED * rows + SEL * FT),
    )

    keys, out_rest = lax.optimization_barrier((keys, out_rest))
    keys, values, queries = kernel_call(
        split_kernel,
        ((ZED * rows, HD), (ZED * rows, HD), (ZED, rows, HD)),
        (where,),
        (keys, *values),
    )
    outs = {}
    for i, d in enumerate(SEND):
        q = queries[d]
        if i >= 4:
            q = after(q, outs, (SEND[i - 4],))
        o = kernel_call(main_kernel, (rows, HD), (), (q, keys, values, cached), cost(rows, ZED * rows + SEL * FT))
        outs[d] = shifted(o, ZED - d) if d else o

    out_rest = exchanged(out_rest.reshape(ZED, share, HD), "z")
    out_rest = jnp.concatenate([out_rest[0::2], out_rest[1::2]], axis=2)
    out_rest = exchanged(out_rest, "h")
    return kernel_call(
        join_kernel, (rows, MAIN + REST), (where,), [outs[d] for d in range(ZED)] + [out_rest]
    )


def solution(mesh):
    grid = Mesh(mesh.devices.reshape(CAND, ZED, GROUP), ("cand", "z", "h"))
    tokens = P(("cand", "z"), "h")
    placed = (
        tokens,
        tokens,
        tokens,
        P("h"),
        P("h"),
        P(("cand", "z"), None, None, "h"),
        P(),
        P(),
    )
    return jax.shard_map(body, mesh=grid, in_specs=placed, out_specs=tokens, check_vma=False)
```
